32 devices in a mesh: grp: 4 (over y, core), head: 8 (over z, x).
Axes of the slice: x: 2, y: 2, z: 4, core: 2. Of those that a mesh axis runs over, the one named last changes fastest.
Arguments:
- query_latent: bfloat16 [2048, 1536], P('grp'), may hold values from -6 to 6
- q_weight: bfloat16 [1536, 24576], P('grp', 'head'), may hold values from -0.15625 to 0.15625
- key_absorb: bfloat16 [128, 128, 512], P('head'), may hold values from -0.5 to 0.5
- value_up: bfloat16 [128, 512, 128], P('head'), may hold values from -0.25 to 0.25
- branch_latent: bfloat16 [4, 1536, 576], P('grp', 'head'), may hold values from -800 to 800, as said below
- lengths: int32 [4], P('grp'), may hold values from 512 to 1536, as said below
- row_depth: int32 [2048], P('grp'), may hold values from 1 to 1536
Outputs:
- attended: bfloat16 [2048, 16384], P('grp', 'head')
The draws below stay inside these ranges and needn't reach their ends.
Inputs may be any that keep to these rules, and one draw needn't show every extreme that they name: `lengths`: every group has between 512 and 1536 live positions; some group has exactly 1536 and some other exactly 512. `branch_latent`: latent entries of order one.
All inputs are finite; a program needn't handle non-finite values.
Results may differ from the reference program's by a relative error of at most 0.012.
Values may be sent and summed in bfloat16 or wider, within the bound.
A program may use at most 128 MiB of HBM per device.

```python
import jax
import jax.numpy as jnp
from jax import lax

QRANK = 1536
HEADS = 128
NOPE = 128
ROPE = 64
KVR = 512
VDIM = 128
ROWS_GRP = 512
LMAX = 1536
GROUPS = 4
ROWS = 2048


def draw_lengths(key, part):
    inner = jax.random.fold_in(key, 11)
    first, second = jax.random.split(inner)
    base = jax.random.randint(first, (GROUPS,), LMAX // 3, LMAX + 1)
    order = jax.random.permutation(second, GROUPS)
    base = base.at[order[0]].set(LMAX)
    base = base.at[order[1]].set(LMAX // 3)
    return base.astype(jnp.int32)


def draw_branch_latent(key, part):
    inner = jax.random.fold_in(key, 23)
    first = jax.random.fold_in(inner, 0)
    shape = (GROUPS, LMAX, KVR + ROPE)
    base = jnp.clip(jax.random.normal(first, shape, jnp.float32), -6.0, 6.0)
    return base.astype(jnp.bfloat16)


def touch_ends(array, rng, low, largest):
    extent = array.shape
    spot = [jax.random.randint(jax.random.fold_in(rng, axis), (), 0, extent[axis]) for axis in range(len(extent))]
    array = array.at[tuple(spot)].set(low)
    longest = extent.index(max(extent))
    spot[longest] = (spot[longest] + 1) % extent[longest]
    return array.at[tuple(spot)].set(largest)


def shard_levels(stream_key, extent, cuts, smallest, high):
    def one(axis_at, shards_of):
        draws = jax.random.uniform(jax.random.fold_in(jax.random.fold_in(stream_key, 6), axis_at), (shards_of,), jnp.float32, smallest / len(cuts), high / len(cuts))
        return jnp.repeat(jnp.exp(draws), extent[axis_at] // shards_of).reshape((-1,) + (1,) * (len(extent) - axis_at - 1))

    factor_of = one(*cuts[0])
    for cut in cuts[1:]:
        factor_of = factor_of * one(*cut)
    return factor_of


def noise(own_key, shape, spread, reach, cuts=(), held_as=jnp.bfloat16):
    gain = shard_levels(own_key, shape, cuts, -0.22, 0.18) if cuts else 1.0
    drawn = jax.random.normal(own_key, shape, jnp.float32) * spread * gain
    return jnp.minimum(jnp.maximum(drawn, -reach), reach).astype(held_as)


def setup_inputs(seed: int = 0) -> dict:
    keys = jax.random.split(jax.random.key(seed), 8)
    query_latent = noise(keys[0], (ROWS, QRANK), 1.0, 6.0, ((0, 4),))
    q_weight = noise(keys[1], (QRANK, HEADS * (NOPE + ROPE)), QRANK ** -0.5, 0.15625, ((0, 4), (1, 8)))
    key_absorb = noise(keys[2], (HEADS, NOPE, KVR), NOPE ** -0.5, 0.5, ((0, 8),))
    value_up = noise(keys[3], (HEADS, KVR, VDIM), KVR ** -0.5, 0.25, ((0, 8),))
    branch_latent = draw_branch_latent(jax.random.fold_in(keys[7], 71), 0)
    lengths = draw_lengths(jax.random.fold_in(keys[7], 71), 0)
    row_depth = touch_ends(jax.random.randint(keys[6], (ROWS,), 1, LMAX + 1), jax.random.fold_in(keys[6], 1), 1, LMAX).astype(jnp.int32)
    return dict(query_latent=query_latent, q_weight=q_weight, key_absorb=key_absorb, value_up=value_up, branch_latent=branch_latent, lengths=lengths, row_depth=row_depth)


def attend(queries, depth, limit, latent, scale):
    count = queries.shape[0]
    block = 512 if count % 512 == 0 else count
    positions = jnp.arange(latent.shape[0], dtype=jnp.int32)
    values = latent[:, :KVR]
    query_blocks = queries.reshape(count // block, block, queries.shape[1])
    depth_blocks = jnp.minimum(depth, limit).reshape(count // block, block)

    def one_block(pair):
        query_rows, seen = pair
        score = lax.dot_general(query_rows, latent, (((1,), (1,)), ((), ())), preferred_element_type=jnp.float32) * scale
        score = jnp.where(positions[None, :] < seen[:, None], score, jnp.float32(-1e30))
        peak = jnp.max(score, axis=1, keepdims=True)
        expo = jnp.exp(score - peak)
        weights = (expo / jnp.sum(expo, axis=1, keepdims=True)).astype(jnp.bfloat16)
        return jnp.dot(weights, values, preferred_element_type=jnp.float32).astype(jnp.bfloat16)

    result = lax.map(one_block, (query_blocks, depth_blocks))
    return result.reshape(count, values.shape[1])


def reference(query_latent, q_weight, key_absorb, value_up, branch_latent, lengths, row_depth):
    scale = jnp.float32((NOPE + ROPE) ** -0.5)
    query = jnp.dot(query_latent, q_weight, preferred_element_type=jnp.float32).astype(jnp.bfloat16)
    query = query.reshape(ROWS, HEADS, NOPE + ROPE)
    q_lat = jnp.einsum("rhd,hdc->rhc", query[:, :, :NOPE].astype(jnp.float32), key_absorb.astype(jnp.float32)).astype(jnp.bfloat16)
    q_abs = jnp.concatenate([q_lat, query[:, :, NOPE:]], axis=2)
    grouped = q_abs.reshape(GROUPS, ROWS_GRP * HEADS, KVR + ROPE)
    depth = jnp.repeat(row_depth.reshape(GROUPS, ROWS_GRP), HEADS, axis=1)

    def per_group(items):
        queries, seen, limit, latent = items
        return attend(queries, seen, limit, latent, scale)

    context = lax.map(per_group, (grouped, depth, lengths, branch_latent))
    context = context.reshape(ROWS, HEADS, KVR)
    result = jnp.einsum("rhc,hcv->rhv", context.astype(jnp.float32), value_up.astype(jnp.float32))
    return result.reshape(ROWS, HEADS * VDIM).astype(jnp.bfloat16)
```

```python
import functools
import math

import jax
import jax.numpy as jnp
from jax import lax
from jax.experimental import pallas as pl
from jax.experimental.pallas import tpu as pltpu
from jax.sharding import PartitionSpec as P

NOPE = 128
ROPE = 64
KVR = 512
VDIM = 128
HEAD = NOPE + ROPE
PAIR = 2 * HEAD
WIDE = 256
AHEAD = 3
MESH = pl.DeviceIdType.MESH
NT = (((1,), (1,)), ((), ()))
SCALE = (HEAD ** -0.5) * math.log2(math.e)


def kernel(Y, Z, X, ql_h, w_h, ka_h, vu_h, lat_h, dep, lens, out_h,
           wbuf, ql, ka, vu, lat, kt, vv, obuf, qb, seen,
           ysend, yrecv, csend, crecv, fsend, frecv,
           zsend, zrecv, xsend, xrecv, lsem, vsem, osem):
    rows, rank = ql.shape
    depth, cols = w_h.shape
    heads = vu_h.shape[0]
    share = lat_h.shape[0]
    length = lat.shape[0]
    pieces = cols // PAIR
    chunk = 128 * share // math.gcd(128, share)
    chunks = length // chunk
    whole_rows = chunk == X * share
    g, h = lax.axis_index("grp"), lax.axis_index("head")
    y, c = lax.div(g, 2), lax.rem(g, 2)
    z, x = lax.div(h, X), lax.rem(h, X)

    def y_at(d):
        return {"grp": lax.rem(y + d, Y) * 2 + c, "head": h}

    other = {"grp": y * 2 + 1 - c, "head": h}

    def z_at(d):
        return {"grp": g, "head": lax.rem(z + d, Z) * X + x}

    def x_at(d):
        return {"grp": g, "head": z * X + lax.rem(x + d, X)}

    def w_part(owner, j):
        return wbuf.at[pl.ds(pl.multiple_of(owner * depth, 16), depth),
                       pl.ds(pl.multiple_of(j * PAIR, 128), PAIR)]

    def w_own(j):
        return w_h.at[:, pl.ds(pl.multiple_of(j * PAIR, 128), PAIR)]

    def shard(index):
        return lat.at[pl.ds(pl.multiple_of(index * share, 16), share)]

    def remote(src, dst, send, recv, to):
        return pltpu.make_async_remote_copy(
            src_ref=src, dst_ref=dst, send_sem=send, recv_sem=recv,
            device_id=to, device_id_type=MESH)

    def y_copy(j, d):
        return remote(w_own(j), w_part(g, j), ysend.at[d - 1, j], yrecv.at[d - 1, j], y_at(d))

    def c_copy(j):
        return remote(w_own(j), w_part(g, j), csend.at[j], crecv.at[j], other)

    def f_copy(j, d):
        part = w_part(lax.rem(y + Y - d, Y) * 2 + c, j)
        return remote(part, part, fsend.at[d - 1, j], frecv.at[d - 1, j], other)

    def z_copy(d):
        return remote(lat_h, shard(h), zsend.at[d - 1], zrecv.at[d - 1], z_at(d))

    def x_copy(dz, dx):
        if dz == 0:
            src, dst = lat_h, shard(h)
        else:
            src = dst = shard(lax.rem(z + Z - dz, Z) * X + x)
        return remote(src, dst, xsend.at[dz, dx - 1], xrecv.at[dz, dx - 1], x_at(dx))

    peers = ([y_at(d) for d in range(1, Y)] + [other]
             + [z_at(d) for d in range(1, Z)] + [x_at(d) for d in range(1, X)])
    barrier = pltpu.get_barrier_semaphore()
    for peer in peers:
        pl.semaphore_signal(barrier, inc=1, device_id=peer, device_id_type=MESH)

    local = [
        pltpu.make_async_copy(lat_h, shard(h), lsem.at[0]),
        pltpu.make_async_copy(ka_h, ka, lsem.at[1]),
        pltpu.make_async_copy(ql_h, ql, lsem.at[2]),
        pltpu.make_async_copy(w_h, wbuf.at[pl.ds(pl.multiple_of(g * depth, 16), depth)], lsem.at[3]),
    ]
    for i in range(heads):
        local.append(pltpu.make_async_copy(vu_h.at[i], vu.at[:, pl.ds(i * VDIM, VDIM)], vsem.at[i]))
    for copy in local:
        copy.start()
    pl.semaphore_wait(barrier, len(peers))

    def start_piece(j):
        for d in range(1, Y):
            y_copy(j, d).start()
        c_copy(j).start()

    start_piece(0)
    for dx in range(1, X):
        x_copy(0, dx).start()
    for d in range(1, Z):
        z_copy(d).start()
    for j in range(1, min(AHEAD, pieces)):
        start_piece(j)

    row = lax.broadcasted_iota(jnp.int32, (rows, rows), 0)
    col = lax.broadcasted_iota(jnp.int32, (rows, rows), 1)
    kept = jnp.minimum(dep[...], lens[0]).astype(jnp.float32)
    seen[...] = jnp.sum(jnp.where(row == col, kept, 0.0), axis=1, keepdims=True).astype(jnp.int32)

    for copy in local:
        copy.wait()

    eye = (lax.broadcasted_iota(jnp.int32, (ROPE, ROPE), 0)
           == lax.broadcasted_iota(jnp.int32, (ROPE, ROPE), 1)).astype(jnp.bfloat16)
    at_once = 4

    def keys_values(index):
        at = pl.ds(pl.multiple_of(index * chunk, 128), chunk)
        rope = lax.dot_general(eye, lat[at, KVR:], NT, preferred_element_type=jnp.float32).astype(jnp.bfloat16)
        blank = jnp.zeros((ROPE, chunk), jnp.bfloat16)

        @pl.loop(0, heads // at_once)
        def _(i):
            latent = lat[at, :KVR]
            wide = at_once * NOPE
            keys = lax.dot_general(ka[pl.ds(pl.multiple_of(i * wide, 16), wide), :], latent, NT,
                                   preferred_element_type=jnp.float32).astype(jnp.bfloat16)
            for e in range(at_once):
                own = keys[e * NOPE:(e + 1) * NOPE]
                head = i * at_once + e
                if e % 2 == 0:
                    kt[head, 0:NOPE, at] = own
                    kt[head, NOPE:HEAD, at] = rope
                    kt[head, HEAD:WIDE, at] = blank
                else:
                    kt[head, 0:ROPE, at] = blank
                    kt[head, ROPE:HEAD, at] = own
                    kt[head, HEAD:WIDE, at] = rope
            over = pl.ds(pl.multiple_of(i * wide, 128), wide)
            vv[at, over] = jnp.dot(latent, vu[:, over], preferred_element_type=jnp.float32).astype(jnp.bfloat16)

    def take_x(dz):
        for dx in range(1, X):
            x_copy(dz, dx).wait_recv()

    def pass_on(dz):
        z_copy(dz).wait_recv()
        for dx in range(1, X):
            x_copy(dz, dx).start()

    waited = 0
    started = min(AHEAD, pieces)
    if not whole_rows:
        for dz in range(1, Z):
            pass_on(dz)
        for dz in range(Z):
            take_x(dz)
    for k in range(chunks):
        if whole_rows:
            if k + 1 < Z:
                pass_on(k + 1)
            take_x(k)
            keys_values(lax.rem(z + Z - k, Z))
        else:
            keys_values(k)
        if started < pieces:
            for d in range(1, Y):
                y_copy(waited, d).wait_send()
            waited += 1
            start_piece(started)
            started += 1
    while started < pieces:
        start_piece(started)
        started += 1

    half = rows // 2
    ones = jnp.ones((length, VDIM), jnp.bfloat16)

    @pl.loop(0, pieces)
    def _(j):
        for d in range(1, Y):
            y_copy(j, d).wait_recv()
            f_copy(j, d).start()
        c_copy(j).wait_recv()
        for d in range(1, Y):
            f_copy(j, d).wait_recv()
        weight = pl.ds(pl.multiple_of(j * PAIR, 128), PAIR)
        for r in range(2):
            part = slice(r * half, (r + 1) * half)
            q = jnp.dot(ql[part, :], wbuf[:, weight], preferred_element_type=jnp.float32)
            qb[part, :] = (q * jnp.float32(SCALE)).astype(jnp.bfloat16)
        for r in range(2):
            part = slice(r * half, (r + 1) * half)
            limit = seen[part, :]
            for e in range(2):
                head = j * 2 + e
                q = qb[part, 0:WIDE] if e == 0 else qb[part, NOPE:PAIR]
                s = jnp.dot(q, kt[head], preferred_element_type=jnp.float32)
                place = lax.broadcasted_iota(jnp.int32, s.shape, 1)
                s = jnp.where(place < limit, s, jnp.float32(-1e30))
                peak = jnp.max(s, axis=1, keepdims=True)
                p = jnp.exp2(s - peak).astype(jnp.bfloat16)
                over = pl.ds(pl.multiple_of(head * VDIM, 128), VDIM)
                both = jnp.concatenate([vv[:, over], ones], axis=1)
                acc = jnp.dot(p, both, preferred_element_type=jnp.float32)
                obuf[part, over] = (acc[:, :VDIM] / acc[:, VDIM:]).astype(jnp.bfloat16)
        done = pl.ds(pl.multiple_of(j * 2 * VDIM, 128), 2 * VDIM)
        pltpu.make_async_copy(obuf.at[:, done], out_h.at[:, done], osem.at[j]).start()

    for dz in range(1, Z):
        z_copy(dz).wait_send()
    for dz in range(Z):
        for dx in range(1, X):
            x_copy(dz, dx).wait_send()

    for j in range(waited, pieces):
        for d in range(1, Y):
            y_copy(j, d).wait_send()

    @pl.loop(0, pieces)
    def _(j):
        c_copy(j).wait_send()
        for d in range(1, Y):
            f_copy(j, d).wait_send()
        done = pl.ds(pl.multiple_of(j * 2 * VDIM, 128), 2 * VDIM)
        pltpu.make_async_copy(obuf.at[:, done], out_h.at[:, done], osem.at[j]).wait()


def per_device(Y, Z, X, query_latent, q_weight, key_absorb, value_up, branch_latent, lengths, row_depth):
    rows, rank = query_latent.shape
    cols = q_weight.shape[1]
    heads = key_absorb.shape[0]
    share = branch_latent.shape[1]
    length = share * Z * X
    pieces = cols // PAIR
    width = heads * VDIM
    bf = jnp.bfloat16
    dma = pltpu.SemaphoreType.DMA
    anywhere = pl.BlockSpec(memory_space=pl.ANY)
    return pl.pallas_call(
        functools.partial(kernel, Y, Z, X),
        out_shape=jax.ShapeDtypeStruct((rows, width), bf),
        in_specs=[anywhere] * 5 + [pl.BlockSpec(memory_space=pltpu.VMEM), pl.BlockSpec(memory_space=pltpu.SMEM)],
        out_specs=anywhere,
        scratch_shapes=[
            pltpu.VMEM((rank, cols), bf),
            pltpu.VMEM((rows, rank), bf),
            pltpu.VMEM((heads * NOPE, KVR), bf),
            pltpu.VMEM((KVR, width), bf),
            pltpu.VMEM((length, KVR + ROPE), bf),
            pltpu.VMEM((heads, WIDE, length), bf),
            pltpu.VMEM((length, width), bf),
            pltpu.VMEM((rows, width), bf),
            pltpu.VMEM((rows, PAIR), bf),
            pltpu.VMEM((rows, 1), jnp.int32),
            dma((Y - 1, pieces)), dma((Y - 1, pieces)),
            dma((pieces,)), dma((pieces,)),
            dma((Y - 1, pieces)), dma((Y - 1, pieces)),
            dma((Z - 1,)), dma((Z - 1,)),
            dma((Z, X - 1)), dma((Z, X - 1)),
            dma((4,)), dma((heads,)), dma((pieces,)),
        ],
        compiler_params=pltpu.CompilerParams(
            collective_id=0, has_side_effects=True, vmem_limit_bytes=60 * 1024 * 1024),
    )(query_latent, q_weight, key_absorb.reshape(heads * NOPE, KVR), value_up,
      branch_latent.reshape(share, KVR + ROPE), row_depth.reshape(1, rows), lengths)


def solution(mesh):
    placed = (
        P("grp", None),
        P("grp", "head"),
        P("head", None, None),
        P("head", None, None),
        P("grp", "head", None),
        P("grp"),
        P("grp"),
    )
    across = math.isqrt(mesh.shape["head"] // 2)
    return jax.shard_map(
        functools.partial(per_device, mesh.shape["grp"] // 2, mesh.shape["head"] // across, across),
        mesh=mesh, in_specs=placed, out_specs=P("grp", "head"), check_vma=False
    )
```

```python
import functools
import math

import jax
import jax.numpy as jnp
from jax import lax
from jax.experimental import pallas as pl
from jax.experimental.pallas import tpu as pltpu
from jax.sharding import PartitionSpec as P

NOPE = 128
ROPE = 64
KVR = 512
VDIM = 128
HEAD = NOPE + ROPE
PAIR = 2 * HEAD
WIDE = 256
AHEAD = 3
MESH = pl.DeviceIdType.MESH
NT = (((1,), (1,)), ((), ()))
SCALE = (HEAD ** -0.5) * math.log2(math.e)


def kernel(Y, Z, X, ql_h, w_h, ka_h, vu_h, lat_h, dep, lens, out_h,
           wbuf, ql, ka, vu, vut, lat, kx, vt, obuf, qb, bias,
           ysend, yrecv, csend, crecv, fsend, frecv,
           zsend, zrecv, xsend, xrecv, lsem, vsem, osem):
    rows, rank = ql.shape
    depth, cols = w_h.shape
    heads = vu.shape[0]
    share = lat_h.shape[0]
    length = lat.shape[0]
    pieces = cols // PAIR
    chunk = 128 * share // math.gcd(128, share)
    chunks = length // chunk
    whole_rows = chunk == X * share
    g, h = lax.axis_index("grp"), lax.axis_index("head")
    y, c = lax.div(g, 2), lax.rem(g, 2)
    z, x = lax.div(h, X), lax.rem(h, X)

    def y_at(d):
        return {"grp": lax.rem(y + d, Y) * 2 + c, "head": h}

    other = {"grp": y * 2 + 1 - c, "head": h}

    def z_at(d):
        return {"grp": g, "head": lax.rem(z + d, Z) * X + x}

    def x_at(d):
        return {"grp": g, "head": z * X + lax.rem(x + d, X)}

    def w_part(owner, j):
        return wbuf.at[pl.ds(pl.multiple_of(owner * depth, 16), depth),
                       pl.ds(pl.multiple_of(j * PAIR, 128), PAIR)]

    def w_own(j):
        return w_h.at[:, pl.ds(pl.multiple_of(j * PAIR, 128), PAIR)]

    def shard(index):
        return lat.at[pl.ds(pl.multiple_of(index * share, 16), share)]

    def remote(src, dst, send, recv, to):
        return pltpu.make_async_remote_copy(
            src_ref=src, dst_ref=dst, send_sem=send, recv_sem=recv,
            device_id=to, device_id_type=MESH)

    def y_copy(j, d):
        return remote(w_own(j), w_part(g, j), ysend.at[d - 1, j], yrecv.at[d - 1, j], y_at(d))

    def c_copy(j):
        return remote(w_own(j), w_part(g, j), csend.at[j], crecv.at[j], other)

    def f_copy(j, d):
        part = w_part(lax.rem(y + Y - d, Y) * 2 + c, j)
        return remote(part, part, fsend.at[d - 1, j], frecv.at[d - 1, j], other)

    def z_copy(d):
        return remote(lat_h, shard(h), zsend.at[d - 1], zrecv.at[d - 1], z_at(d))

    def x_copy(dz, dx):
        if dz == 0:
            src, dst = lat_h, shard(h)
        else:
            src = dst = shard(lax.rem(z + Z - dz, Z) * X + x)
        return remote(src, dst, xsend.at[dz, dx - 1], xrecv.at[dz, dx - 1], x_at(dx))

    peers = ([y_at(d) for d in range(1, Y)] + [other]
             + [z_at(d) for d in range(1, Z)] + [x_at(d) for d in range(1, X)])
    barrier = pltpu.get_barrier_semaphore()
    for peer in peers:
        pl.semaphore_signal(barrier, inc=1, device_id=peer, device_id_type=MESH)

    local = [
        pltpu.make_async_copy(lat_h, shard(h), lsem.at[0]),
        pltpu.make_async_copy(vu_h, vu, lsem.at[1]),
        pltpu.make_async_copy(ql_h, ql, lsem.at[2]),
        pltpu.make_async_copy(w_h, wbuf.at[pl.ds(pl.multiple_of(g * depth, 16), depth)], lsem.at[3]),
    ]
    for i in range(heads):
        for e in range(2):
            src = (e + i) % 2
            local.append(pltpu.make_async_copy(
                ka_h.at[pl.ds(i * NOPE + src * ROPE, ROPE)],
                ka.at[pl.ds(i * NOPE + e * ROPE, ROPE)], vsem.at[2 * i + e]))
    for copy in local:
        copy.start()
    pl.semaphore_wait(barrier, len(peers))

    def start_piece(j):
        for d in range(1, Y):
            y_copy(j, d).start()
        c_copy(j).start()

    start_piece(0)
    for dx in range(1, X):
        x_copy(0, dx).start()
    for d in range(1, Z):
        z_copy(d).start()
    for j in range(1, min(AHEAD, pieces)):
        start_piece(j)

    kept = jnp.minimum(dep[...], lens[0])
    step = 128

    @pl.loop(0, length // step)
    def _(i):
        at = pl.ds(pl.multiple_of(i * step, step), step)
        place = lax.broadcasted_iota(jnp.int32, (step, rows), 0) + i * step
        bias[at, :] = jnp.where(place < kept, 0.0, jnp.float32(-1e30))

    for copy in local:
        copy.wait()

    @pl.loop(0, heads)
    def _(i):
        vut[pl.ds(pl.multiple_of(i * VDIM, 16), VDIM), :] = vu[i].T

    source = lax.broadcasted_iota(jnp.int32, (ROPE, WIDE), 0)
    target = lax.broadcasted_iota(jnp.int32, (ROPE, WIDE), 1)
    spread = ((source == target) | (source + WIDE - ROPE == target)).astype(jnp.bfloat16)
    at_once = 4

    def keys_values(index):
        at = pl.ds(pl.multiple_of(index * chunk, 128), chunk)
        rope = jnp.dot(lat[at, KVR:], spread, preferred_element_type=jnp.float32)
        first = rope[:, :NOPE].astype(jnp.bfloat16)
        low = lax.broadcasted_iota(jnp.int32, (chunk, NOPE), 1) < ROPE

        @pl.loop(0, heads // at_once)
        def _(i):
            latent = lat[at, :KVR]
            wide = at_once * NOPE
            over = pl.ds(pl.multiple_of(i * wide, 128), wide)
            keys = lax.dot_general(latent, ka[over, :], NT, preferred_element_type=jnp.float32)
            for e in range(at_once):
                own = keys[:, e * NOPE:(e + 1) * NOPE]
                base = (i * at_once + e) * WIDE
                left = pl.ds(pl.multiple_of(base, 128), NOPE)
                right = pl.ds(pl.multiple_of(base + NOPE, 128), NOPE)
                if e % 2 == 0:
                    kx[at, left] = own.astype(jnp.bfloat16)
                    kx[at, right] = first
                else:
                    kx[at, left] = jnp.where(low, 0.0, own).astype(jnp.bfloat16)
                    kx[at, right] = jnp.where(low, own, rope[:, NOPE:]).astype(jnp.bfloat16)
            vt[over, at] = lax.dot_general(vut[over, :], latent, NT,
                                           preferred_element_type=jnp.float32).astype(jnp.bfloat16)

    def take_x(dz):
        for dx in range(1, X):
            x_copy(dz, dx).wait_recv()

    def pass_on(dz):
        z_copy(dz).wait_recv()
        for dx in range(1, X):
            x_copy(dz, dx).start()

    half = rows // 2

    def hand_on(j):
        for d in range(1, Y):
            y_copy(j, d).wait_recv()
            f_copy(j, d).start()

    def project(j):
        c_copy(j).wait_recv()
        for d in range(1, Y):
            f_copy(j, d).wait_recv()
        weight = pl.ds(pl.multiple_of(j * PAIR, 128), PAIR)
        q = jnp.dot(ql[...], wbuf[:, weight], preferred_element_type=jnp.float32)
        qb[:, weight] = (q * jnp.float32(SCALE)).astype(jnp.bfloat16)

    waited = 0
    started = min(AHEAD, pieces)
    early = min(chunks - 1, pieces - 1)
    if not whole_rows:
        for dz in range(1, Z):
            pass_on(dz)
        for dz in range(Z):
            take_x(dz)
    for k in range(chunks):
        if whole_rows:
            if k + 1 < Z:
                pass_on(k + 1)
            take_x(k)
        if 1 <= k <= early:
            hand_on(k - 1)
        keys_values(lax.rem(z + Z - k, Z) if whole_rows else k)
        if 1 <= k <= early:
            project(k - 1)
        if started < pieces:
            for d in range(1, Y):
                y_copy(waited, d).wait_send()
            waited += 1
            start_piece(started)
            started += 1
    while started < pieces:
        start_piece(started)
        started += 1

    ones = jnp.ones((16, length), jnp.bfloat16)

    @pl.loop(0, pieces)
    def _(j):
        @pl.when((j + 1 >= early) & (j + 1 < pieces - 1))
        def _():
            hand_on(j + 1)

        @pl.when(j == pieces - 1)
        def _():
            hand_on(j)

        @pl.when(j >= early)
        def _():
            project(j)

        blocks = [(r, e) for r in range(2) for e in range(2)]

        def scores(r, e):
            query = qb[r * half:(r + 1) * half, pl.ds(pl.multiple_of(j * PAIR + e * NOPE, 128), WIDE)]
            key = kx[:, pl.ds(pl.multiple_of((j * 2 + e) * WIDE, 128), WIDE)]
            return lax.dot_general(key, query, NT, preferred_element_type=jnp.float32)

        ahead = scores(*blocks[0])
        for i, (r, e) in enumerate(blocks):
            s = ahead
            if i + 1 < len(blocks):
                ahead = scores(*blocks[i + 1])
            part = slice(r * half, (r + 1) * half)
            s = s + bias[:, part]
            peak = jnp.max(s, axis=0, keepdims=True)
            p = jnp.exp2(s - peak).astype(jnp.bfloat16)
            over = pl.ds(pl.multiple_of((j * 2 + e) * VDIM, 128), VDIM)
            both = jnp.concatenate([vt[over, :], ones], axis=0)
            acc = jnp.dot(both, p, preferred_element_type=jnp.float32)
            obuf[part, over] = (acc[:VDIM] / acc[VDIM:VDIM + 1]).T.astype(jnp.bfloat16)
        done = pl.ds(pl.multiple_of(j * 2 * VDIM, 128), 2 * VDIM)
        pltpu.make_async_copy(obuf.at[:, done], out_h.at[:, done], osem.at[j]).start()

    for dz in range(1, Z):
        z_copy(dz).wait_send()
    for dz in range(Z):
        for dx in range(1, X):
            x_copy(dz, dx).wait_send()

    for j in range(waited, pieces):
        for d in range(1, Y):
            y_copy(j, d).wait_send()

    @pl.loop(0, pieces)
    def _(j):
        c_copy(j).wait_send()
        for d in range(1, Y):
            f_copy(j, d).wait_send()
        done = pl.ds(pl.multiple_of(j * 2 * VDIM, 128), 2 * VDIM)
        pltpu.make_async_copy(obuf.at[:, done], out_h.at[:, done], osem.at[j]).wait()


def per_device(Y, Z, X, query_latent, q_weight, key_absorb, value_up, branch_latent, lengths, row_depth):
    rows, rank = query_latent.shape
    cols = q_weight.shape[1]
    heads = key_absorb.shape[0]
    share = branch_latent.shape[1]
    length = share * Z * X
    pieces = cols // PAIR
    width = heads * VDIM
    bf = jnp.bfloat16
    dma = pltpu.SemaphoreType.DMA
    anywhere = pl.BlockSpec(memory_space=pl.ANY)
    return pl.pallas_call(
        functools.partial(kernel, Y, Z, X),
        out_shape=jax.ShapeDtypeStruct((rows, width), bf),
        in_specs=[anywhere] * 5 + [pl.BlockSpec(memory_space=pltpu.VMEM), pl.BlockSpec(memory_space=pltpu.SMEM)],
        out_specs=anywhere,
        scratch_shapes=[
            pltpu.VMEM((rank, cols), bf),
            pltpu.VMEM((rows, rank), bf),
            pltpu.VMEM((heads * NOPE, KVR), bf),
            pltpu.VMEM((heads, KVR, VDIM), bf),
            pltpu.VMEM((width, KVR), bf),
            pltpu.VMEM((length, KVR + ROPE), bf),
            pltpu.VMEM((length, heads * WIDE), bf),
            pltpu.VMEM((width, length), bf),
            pltpu.VMEM((rows, width), bf),
            pltpu.VMEM((rows, cols), bf),
            pltpu.VMEM((length, rows), jnp.float32),
            dma((Y - 1, pieces)), dma((Y - 1, pieces)),
            dma((pieces,)), dma((pieces,)),
            dma((Y - 1, pieces)), dma((Y - 1, pieces)),
            dma((Z - 1,)), dma((Z - 1,)),
            dma((Z, X - 1)), dma((Z, X - 1)),
            dma((4,)), dma((2 * heads,)), dma((pieces,)),
        ],
        compiler_params=pltpu.CompilerParams(
            collective_id=0, has_side_effects=True, vmem_limit_bytes=60 * 1024 * 1024),
    )(query_latent, q_weight, key_absorb.reshape(heads * NOPE, KVR), value_up,
      branch_latent.reshape(share, KVR + ROPE), row_depth.reshape(1, rows), lengths)


def solution(mesh):
    placed = (
        P("grp", None),
        P("grp", "head"),
        P("head", None, None),
        P("head", None, None),
        P("grp", "head", None),
        P("grp"),
        P("grp"),
    )
    across = math.isqrt(mesh.shape["head"] // 2)
    return jax.shard_map(
        functools.partial(per_device, mesh.shape["grp"] // 2, mesh.shape["head"] // across, across),
        mesh=mesh, in_specs=placed, out_specs=P("grp", "head"), check_vma=False
    )
```

```python
import functools
import math

import jax
import jax.numpy as jnp
from jax import lax
from jax.experimental import pallas as pl
from jax.experimental.pallas import tpu as pltpu
from jax.sharding import PartitionSpec as P

NOPE = 128
ROPE = 64
KVR = 512
VDIM = 128
HEAD = NOPE + ROPE
PAIR = 2 * HEAD
WIDE = 256
AHEAD = 4
MESH = pl.DeviceIdType.MESH
NT = (((1,), (1,)), ((), ()))
SCALE = (HEAD ** -0.5) * math.log2(math.e)


def kernel(Y, Z, X, ql_h, w_h, ka_h, vu_h, lat_h, dep, lens, out_h,
           wbuf, ql, ka, vu, vut, lat, kx, vt, obuf, qb, bias,
           ysend, yrecv, csend, crecv, fsend, frecv,
           upsend, uprecv, downsend, downrecv, xsend, xrecv, lsem, vsem, osem):
    rows, rank = ql.shape
    depth, cols = w_h.shape
    heads = vu.shape[0]
    share = lat_h.shape[0]
    length = lat.shape[0]
    pieces = cols // PAIR
    chunk = 128 * share // math.gcd(128, share)
    chunks = length // chunk
    whole_rows = chunk == X * share
    g, h = lax.axis_index("grp"), lax.axis_index("head")
    y, c = lax.div(g, 2), lax.rem(g, 2)
    z, x = lax.div(h, X), lax.rem(h, X)

    def y_at(d):
        return {"grp": lax.rem(y + d, Y) * 2 + c, "head": h}

    other = {"grp": y * 2 + 1 - c, "head": h}

    def z_at(d):
        return {"grp": g, "head": lax.rem(z + d, Z) * X + x}

    def x_at(d):
        return {"grp": g, "head": z * X + lax.rem(x + d, X)}

    def w_part(owner, j):
        return wbuf.at[pl.ds(pl.multiple_of(owner * depth, 16), depth),
                       pl.ds(pl.multiple_of(j * PAIR, 128), PAIR)]

    def w_own(j):
        return w_h.at[:, pl.ds(pl.multiple_of(j * PAIR, 128), PAIR)]

    def shard(index):
        return lat.at[pl.ds(pl.multiple_of(index * share, 16), share)]

    def remote(src, dst, send, recv, to):
        return pltpu.make_async_remote_copy(
            src_ref=src, dst_ref=dst, send_sem=send, recv_sem=recv,
            device_id=to, device_id_type=MESH)

    def y_copy(j, d):
        return remote(w_own(j), w_part(g, j), ysend.at[d - 1, j], yrecv.at[d - 1, j], y_at(d))

    def c_copy(j):
        return remote(w_own(j), w_part(g, j), csend.at[j], crecv.at[j], other)

    def f_copy(j, d):
        part = w_part(lax.rem(y + Y - d, Y) * 2 + c, j)
        return remote(part, part, fsend.at[d - 1, j], frecv.at[d - 1, j], other)

    def up_copy(t):
        part = shard((z - t + 1) * X + x)
        return remote(lat_h if t == 1 else part, part, upsend.at[t - 1], uprecv.at[t - 1], z_at(1))

    def down_copy(t):
        part = shard((z + t - 1) * X + x)
        return remote(lat_h if t == 1 else part, part, downsend.at[t - 1], downrecv.at[t - 1], z_at(Z - 1))

    def x_copy(layer, dx, own=False):
        part = shard(layer * X + x)
        return remote(lat_h if own else part, part, xsend.at[layer, dx - 1], xrecv.at[layer, dx - 1], x_at(dx))

    def sends_up(t):
        return (z - t + 1 >= 0) & (z + 1 < Z)

    def sends_down(t):
        return (z + t - 1 < Z) & (z >= 1)

    peers = ([y_at(d) for d in range(1, Y)] + [other]
             + [z_at(d) for d in range(1, Z)] + [x_at(d) for d in range(1, X)])
    barrier = pltpu.get_barrier_semaphore()
    for peer in peers:
        pl.semaphore_signal(barrier, inc=1, device_id=peer, device_id_type=MESH)

    local = [
        pltpu.make_async_copy(lat_h, shard(h), lsem.at[0]),
        pltpu.make_async_copy(vu_h, vu, lsem.at[1]),
        pltpu.make_async_copy(ql_h, ql, lsem.at[2]),
        pltpu.make_async_copy(w_h, wbuf.at[pl.ds(pl.multiple_of(g * depth, 16), depth)], lsem.at[3]),
    ]
    for i in range(heads):
        for e in range(2):
            src = (e + i) % 2
            local.append(pltpu.make_async_copy(
                ka_h.at[pl.ds(i * NOPE + src * ROPE, ROPE)],
                ka.at[pl.ds(i * NOPE + e * ROPE, ROPE)], vsem.at[2 * i + e]))
    for copy in local:
        copy.start()
    pl.semaphore_wait(barrier, len(peers))

    def start_piece(j):
        for d in range(1, Y):
            y_copy(j, d).start()
        c_copy(j).start()

    start_piece(0)
    for dx in range(1, X):
        x_copy(z, dx, True).start()

    def pass_up(t):
        @pl.when(sends_up(t))
        def _():
            up_copy(t).start()

    def pass_down(t):
        @pl.when(sends_down(t))
        def _():
            down_copy(t).start()

    pass_up(1)
    pass_down(1)
    for j in range(1, min(AHEAD, pieces)):
        start_piece(j)

    kept = jnp.minimum(dep[...], lens[0])
    step = 128

    @pl.loop(0, length // step)
    def _(i):
        at = pl.ds(pl.multiple_of(i * step, step), step)
        place = lax.broadcasted_iota(jnp.int32, (step, rows), 0) + i * step
        bias[at, :] = jnp.where(place < kept, 0.0, jnp.float32(-1e30))

    for copy in local:
        copy.wait()

    @pl.loop(0, heads)
    def _(i):
        vut[pl.ds(pl.multiple_of(i * VDIM, 16), VDIM), :] = vu[i].T

    source = lax.broadcasted_iota(jnp.int32, (ROPE, WIDE), 0)
    target = lax.broadcasted_iota(jnp.int32, (ROPE, WIDE), 1)
    spread = ((source == target) | (source + WIDE - ROPE == target)).astype(jnp.bfloat16)
    at_once = 4

    def keys_values(index):
        at = pl.ds(pl.multiple_of(index * chunk, 128), chunk)
        rope = jnp.dot(lat[at, KVR:], spread, preferred_element_type=jnp.float32)
        first = rope[:, :NOPE].astype(jnp.bfloat16)
        low = lax.broadcasted_iota(jnp.int32, (chunk, NOPE), 1) < ROPE

        @pl.loop(0, heads // at_once)
        def _(i):
            latent = lat[at, :KVR]
            wide = at_once * NOPE
            over = pl.ds(pl.multiple_of(i * wide, 128), wide)
            keys = lax.dot_general(latent, ka[over, :], NT, preferred_element_type=jnp.float32)
            for e in range(at_once):
                own = keys[:, e * NOPE:(e + 1) * NOPE]
                base = (i * at_once + e) * WIDE
                left = pl.ds(pl.multiple_of(base, 128), NOPE)
                right = pl.ds(pl.multiple_of(base + NOPE, 128), NOPE)
                if e % 2 == 0:
                    kx[at, left] = own.astype(jnp.bfloat16)
                    kx[at, right] = first
                else:
                    kx[at, left] = jnp.where(low, 0.0, own).astype(jnp.bfloat16)
                    kx[at, right] = jnp.where(low, own, rope[:, NOPE:]).astype(jnp.bfloat16)
            vt[over, at] = lax.dot_general(vut[over, :], latent, NT,
                                           preferred_element_type=jnp.float32).astype(jnp.bfloat16)

    def take_x(layer):
        for dx in range(1, X):
            x_copy(layer, dx).wait_recv()

    def relay(t):
        @pl.when(z - t >= 0)
        def _():
            up_copy(t).wait_recv()
            if t + 1 < Z:
                pass_up(t + 1)
            for dx in range(1, X):
                x_copy(z - t, dx).start()

        @pl.when(z + t < Z)
        def _():
            down_copy(t).wait_recv()
            if t + 1 < Z:
                pass_down(t + 1)
            for dx in range(1, X):
                x_copy(z + t, dx).start()

    def layers(t):
        @pl.when(z - t >= 0)
        def _():
            take_x(z - t)
            keys_values(z - t)

        @pl.when(z + t < Z)
        def _():
            take_x(z + t)
            keys_values(z + t)

    half = rows // 2

    def hand_on(j):
        for d in range(1, Y):
            y_copy(j, d).wait_recv()
            f_copy(j, d).start()

    def project(j):
        c_copy(j).wait_recv()
        for d in range(1, Y):
            f_copy(j, d).wait_recv()
        weight = pl.ds(pl.multiple_of(j * PAIR, 128), PAIR)
        q = jnp.dot(ql[...], wbuf[:, weight], preferred_element_type=jnp.float32)
        qb[:, weight] = (q * jnp.float32(SCALE)).astype(jnp.bfloat16)

    started = min(AHEAD, pieces)
    early = min(2, pieces - 1)
    take_x(z)
    if whole_rows:
        relay(1)
        keys_values(z)
        for t in range(1, Z):
            if t + 1 < Z:
                relay(t + 1)
            if started < pieces:
                start_piece(started)
                started += 1
            layers(t)
    else:
        for t in range(1, Z):
            relay(t)
        for layer in range(Z):
            @pl.when(z != layer)
            def _():
                take_x(layer)
        for k in range(chunks):
            keys_values(k)
    while started < pieces:
        start_piece(started)
        started += 1
    for j in range(early):
        hand_on(j)
    for j in range(early):
        project(j)

    ones = jnp.ones((16, length), jnp.bfloat16)

    @pl.loop(0, pieces)
    def _(j):
        @pl.when((j + 1 >= early) & (j + 1 < pieces - 1))
        def _():
            hand_on(j + 1)

        @pl.when(j == pieces - 1)
        def _():
            hand_on(j)

        @pl.when(j >= early)
        def _():
            project(j)

        blocks = [(r, e) for r in range(2) for e in range(2)]

        def scores(r, e):
            query = qb[r * half:(r + 1) * half, pl.ds(pl.multiple_of(j * PAIR + e * NOPE, 128), WIDE)]
            key = kx[:, pl.ds(pl.multiple_of((j * 2 + e) * WIDE, 128), WIDE)]
            return lax.dot_general(key, query, NT, preferred_element_type=jnp.float32)

        ahead = scores(*blocks[0])
        for i, (r, e) in enumerate(blocks):
            s = ahead
            if i + 1 < len(blocks):
                ahead = scores(*blocks[i + 1])
            part = slice(r * half, (r + 1) * half)
            s = s + bias[:, part]
            peak = jnp.max(s, axis=0, keepdims=True)
            p = jnp.exp2(s - peak).astype(jnp.bfloat16)
            over = pl.ds(pl.multiple_of((j * 2 + e) * VDIM, 128), VDIM)
            both = jnp.concatenate([vt[over, :], ones], axis=0)
            acc = jnp.dot(both, p, preferred_element_type=jnp.float32)
            obuf[part, over] = (acc[:VDIM] / acc[VDIM:VDIM + 1]).T.astype(jnp.bfloat16)
        done = pl.ds(pl.multiple_of(j * 2 * VDIM, 128), 2 * VDIM)
        pltpu.make_async_copy(obuf.at[:, done], out_h.at[:, done], osem.at[j]).start()

    for t in range(1, Z):
        @pl.when(sends_up(t))
        def _():
            up_copy(t).wait_send()

        @pl.when(sends_down(t))
        def _():
            down_copy(t).wait_send()
    for layer in range(Z):
        for dx in range(1, X):
            x_copy(layer, dx).wait_send()

    @pl.loop(0, pieces)
    def _(j):
        c_copy(j).wait_send()
        for d in range(1, Y):
            y_copy(j, d).wait_send()
            f_copy(j, d).wait_send()
        done = pl.ds(pl.multiple_of(j * 2 * VDIM, 128), 2 * VDIM)
        pltpu.make_async_copy(obuf.at[:, done], out_h.at[:, done], osem.at[j]).wait()


def per_device(Y, Z, X, query_latent, q_weight, key_absorb, value_up, branch_latent, lengths, row_depth):
    rows, rank = query_latent.shape
    cols = q_weight.shape[1]
    heads = key_absorb.shape[0]
    share = branch_latent.shape[1]
    length = share * Z * X
    pieces = cols // PAIR
    width = heads * VDIM
    bf = jnp.bfloat16
    dma = pltpu.SemaphoreType.DMA
    anywhere = pl.BlockSpec(memory_space=pl.ANY)
    return pl.pallas_call(
        functools.partial(kernel, Y, Z, X),
        out_shape=jax.ShapeDtypeStruct((rows, width), bf),
        in_specs=[anywhere] * 5 + [pl.BlockSpec(memory_space=pltpu.VMEM), pl.BlockSpec(memory_space=pltpu.SMEM)],
        out_specs=anywhere,
        scratch_shapes=[
            pltpu.VMEM((rank, cols), bf),
            pltpu.VMEM((rows, rank), bf),
            pltpu.VMEM((heads * NOPE, KVR), bf),
            pltpu.VMEM((heads, KVR, VDIM), bf),
            pltpu.VMEM((width, KVR), bf),
            pltpu.VMEM((length, KVR + ROPE), bf),
            pltpu.VMEM((length, heads * WIDE), bf),
            pltpu.VMEM((width, length), bf),
            pltpu.VMEM((rows, width), bf),
            pltpu.VMEM((rows, cols), bf),
            pltpu.VMEM((length, rows), jnp.float32),
            dma((Y - 1, pieces)), dma((Y - 1, pieces)),
            dma((pieces,)), dma((pieces,)),
            dma((Y - 1, pieces)), dma((Y - 1, pieces)),
            dma((Z - 1,)), dma((Z - 1,)), dma((Z - 1,)), dma((Z - 1,)),
            dma((Z, X - 1)), dma((Z, X - 1)),
            dma((4,)), dma((2 * heads,)), dma((pieces,)),
        ],
        compiler_params=pltpu.CompilerParams(
            collective_id=0, has_side_effects=True, vmem_limit_bytes=60 * 1024 * 1024),
    )(query_latent, q_weight, key_absorb.reshape(heads * NOPE, KVR), value_up,
      branch_latent.reshape(share, KVR + ROPE), row_depth.reshape(1, rows), lengths)


def solution(mesh):
    placed = (
        P("grp", None),
        P("grp", "head"),
        P("head", None, None),
        P("head", None, None),
        P("grp", "head", None),
        P("grp"),
        P("grp"),
    )
    across = math.isqrt(mesh.shape["head"] // 2)
    return jax.shard_map(
        functools.partial(per_device, mesh.shape["grp"] // 2, mesh.shape["head"] // across, across),
        mesh=mesh, in_specs=placed, out_specs=P("grp", "head"), check_vma=False
    )
```

```python
import functools
import math

import jax
import jax.numpy as jnp
from jax import lax
from jax.experimental import pallas as pl
from jax.experimental.pallas import tpu as pltpu
from jax.sharding import PartitionSpec as P

NOPE = 128
ROPE = 64
KVR = 512
VDIM = 128
HEAD = NOPE + ROPE
PAIR = 2 * HEAD
WIDE = 256
AHEAD = 2
LAG = 2
MESH = pl.DeviceIdType.MESH
NT = (((1,), (1,)), ((), ()))
SCALE = (HEAD ** -0.5) * math.log2(math.e)


def kernel(Y, Z, X, ql_h, w_h, ka_h, vu_h, lat_h, dep, lens, out_h,
           wbuf, ql, ka, vu, vut, lat, kx, vt, obuf, qb, bias,
           ysend, yrecv, csend, crecv, fsend, frecv,
           upsend, uprecv, downsend, downrecv, xsend, xrecv, lsem, vsem, osem):
    rows, rank = ql.shape
    depth, cols = w_h.shape
    heads = vu.shape[0]
    share = lat_h.shape[0]
    length = lat.shape[0]
    pieces = cols // PAIR
    chunk = 128 * share // math.gcd(128, share)
    chunks = length // chunk
    whole_rows = chunk == X * share
    g, h = lax.axis_index("grp"), lax.axis_index("head")
    y, c = lax.div(g, 2), lax.rem(g, 2)
    z, x = lax.div(h, X), lax.rem(h, X)

    def y_at(d):
        return {"grp": lax.rem(y + d, Y) * 2 + c, "head": h}

    other = {"grp": y * 2 + 1 - c, "head": h}

    def z_at(d):
        return {"grp": g, "head": lax.rem(z + d, Z) * X + x}

    def x_at(d):
        return {"grp": g, "head": z * X + lax.rem(x + d, X)}

    def w_part(owner, j):
        return wbuf.at[pl.ds(pl.multiple_of(owner * depth, 16), depth),
                       pl.ds(pl.multiple_of(j * PAIR, 128), PAIR)]

    def w_own(j):
        return w_h.at[:, pl.ds(pl.multiple_of(j * PAIR, 128), PAIR)]

    def shard(index):
        return lat.at[pl.ds(pl.multiple_of(index * share, 16), share)]

    def remote(src, dst, send, recv, to):
        return pltpu.make_async_remote_copy(
            src_ref=src, dst_ref=dst, send_sem=send, recv_sem=recv,
            device_id=to, device_id_type=MESH)

    def y_copy(j, d):
        return remote(w_own(j), w_part(g, j), ysend.at[d - 1, j], yrecv.at[d - 1, j], y_at(d))

    def c_copy(j):
        return remote(w_own(j), w_part(g, j), csend.at[j], crecv.at[j], other)

    def f_copy(j, d):
        part = w_part(lax.rem(y + Y - d, Y) * 2 + c, j)
        return remote(part, part, fsend.at[d - 1, j], frecv.at[d - 1, j], other)

    def up_copy(t):
        part = shard((z - t + 1) * X + x)
        return remote(lat_h if t == 1 else part, part, upsend.at[t - 1], uprecv.at[t - 1], z_at(1))

    def down_copy(t):
        part = shard((z + t - 1) * X + x)
        return remote(lat_h if t == 1 else part, part, downsend.at[t - 1], downrecv.at[t - 1], z_at(Z - 1))

    def x_copy(layer, dx, own=False):
        part = shard(layer * X + x)
        return remote(lat_h if own else part, part, xsend.at[layer, dx - 1], xrecv.at[layer, dx - 1], x_at(dx))

    def sends_up(t):
        return (z - t + 1 >= 0) & (z + 1 < Z)

    def sends_down(t):
        return (z + t - 1 < Z) & (z >= 1)

    peers = ([y_at(d) for d in range(1, Y)] + [other]
             + [z_at(d) for d in range(1, Z)] + [x_at(d) for d in range(1, X)])
    barrier = pltpu.get_barrier_semaphore()
    for peer in peers:
        pl.semaphore_signal(barrier, inc=1, device_id=peer, device_id_type=MESH)

    local = [
        pltpu.make_async_copy(lat_h, shard(h), lsem.at[0]),
        pltpu.make_async_copy(vu_h, vu, lsem.at[1]),
        pltpu.make_async_copy(ql_h, ql, lsem.at[2]),
        pltpu.make_async_copy(w_h, wbuf.at[pl.ds(pl.multiple_of(g * depth, 16), depth)], lsem.at[3]),
    ]
    for i in range(heads):
        for e in range(2):
            src = (e + i) % 2
            local.append(pltpu.make_async_copy(
                ka_h.at[pl.ds(i * NOPE + src * ROPE, ROPE)],
                ka.at[pl.ds(i * NOPE + e * ROPE, ROPE)], vsem.at[2 * i + e]))
    for copy in local:
        copy.start()
    pl.semaphore_wait(barrier, len(peers))

    def start_piece(j):
        for d in range(1, Y):
            y_copy(j, d).start()
        c_copy(j).start()

    start_piece(0)
    for dx in range(1, X):
        x_copy(z, dx, True).start()

    def pass_up(t):
        @pl.when(sends_up(t))
        def _():
            up_copy(t).start()

    def pass_down(t):
        @pl.when(sends_down(t))
        def _():
            down_copy(t).start()

    pass_up(1)
    pass_down(1)
    for j in range(1, min(AHEAD, pieces)):
        start_piece(j)

    kept = jnp.minimum(dep[...], lens[0])
    step = 128

    @pl.loop(0, length // step)
    def _(i):
        at = pl.ds(pl.multiple_of(i * step, step), step)
        place = lax.broadcasted_iota(jnp.int32, (step, rows), 0) + i * step
        bias[at, :] = jnp.where(place < kept, 0.0, jnp.float32(-1e30))

    for copy in local:
        copy.wait()

    @pl.loop(0, heads)
    def _(i):
        vut[pl.ds(pl.multiple_of(i * VDIM, 16), VDIM), :] = vu[i].T

    source = lax.broadcasted_iota(jnp.int32, (ROPE, WIDE), 0)
    target = lax.broadcasted_iota(jnp.int32, (ROPE, WIDE), 1)
    spread = ((source == target) | (source + WIDE - ROPE == target)).astype(jnp.bfloat16)
    at_once = 4

    def keys_values(index):
        at = pl.ds(pl.multiple_of(index * chunk, 128), chunk)
        rope = jnp.dot(lat[at, KVR:], spread, preferred_element_type=jnp.float32)
        first = rope[:, :NOPE].astype(jnp.bfloat16)
        low = lax.broadcasted_iota(jnp.int32, (chunk, NOPE), 1) < ROPE

        @pl.loop(0, heads // at_once)
        def _(i):
            latent = lat[at, :KVR]
            wide = at_once * NOPE
            over = pl.ds(pl.multiple_of(i * wide, 128), wide)
            keys = lax.dot_general(latent, ka[over, :], NT, preferred_element_type=jnp.float32)
            for e in range(at_once):
                own = keys[:, e * NOPE:(e + 1) * NOPE]
                base = (i * at_once + e) * WIDE
                left = pl.ds(pl.multiple_of(base, 128), NOPE)
                right = pl.ds(pl.multiple_of(base + NOPE, 128), NOPE)
                if e % 2 == 0:
                    kx[at, left] = own.astype(jnp.bfloat16)
                    kx[at, right] = first
                else:
                    kx[at, left] = jnp.where(low, 0.0, own).astype(jnp.bfloat16)
                    kx[at, right] = jnp.where(low, own, rope[:, NOPE:]).astype(jnp.bfloat16)
            vt[over, at] = lax.dot_general(vut[over, :], latent, NT,
                                           preferred_element_type=jnp.float32).astype(jnp.bfloat16)

    def take_x(layer):
        for dx in range(1, X):
            x_copy(layer, dx).wait_recv()

    def relay(t):
        @pl.when(z - t >= 0)
        def _():
            up_copy(t).wait_recv()
            if t + 1 < Z:
                pass_up(t + 1)
            for dx in range(1, X):
                x_copy(z - t, dx).start()

        @pl.when(z + t < Z)
        def _():
            down_copy(t).wait_recv()
            if t + 1 < Z:
                pass_down(t + 1)
            for dx in range(1, X):
                x_copy(z + t, dx).start()

    def layers(t):
        @pl.when(z - t >= 0)
        def _():
            take_x(z - t)
            keys_values(z - t)

        @pl.when(z + t < Z)
        def _():
            take_x(z + t)
            keys_values(z + t)

    half = rows // 2

    def hand_on(j):
        for d in range(1, Y):
            y_copy(j, d).wait_recv()
            f_copy(j, d).start()

    def project(j):
        c_copy(j).wait_recv()
        for d in range(1, Y):
            f_copy(j, d).wait_recv()
        weight = pl.ds(pl.multiple_of(j * PAIR, 128), PAIR)
        q = jnp.dot(ql[...], wbuf[:, weight], preferred_element_type=jnp.float32)
        qb[:, weight] = (q * jnp.float32(SCALE)).astype(jnp.bfloat16)

    started = min(AHEAD, pieces)
    left = set(range(pieces))

    def next_piece(after):
        nonlocal started
        if started < pieces:
            if after >= 0:
                for d in range(1, Y):
                    y_copy(after, d).wait_send()
                left.discard(after)
            start_piece(started)
            started += 1

    early = min(2, pieces - 1)
    take_x(z)
    if whole_rows:
        relay(1)
        keys_values(z)
        for t in range(1, Z):
            if t + 1 < Z:
                relay(t + 1)
            if t % 2 == 1:
                next_piece(started - 3)
            layers(t)
    else:
        for t in range(1, Z):
            relay(t)
        for layer in range(Z):
            @pl.when(z != layer)
            def _():
                take_x(layer)
        for k in range(chunks):
            keys_values(k)
    next_piece(started - 3)
    for j in range(early):
        hand_on(j)
    for j in range(early):
        project(j)

    ones = jnp.ones((16, length), jnp.bfloat16)

    @pl.loop(0, pieces)
    def _(j):
        @pl.when(j >= early)
        def _():
            project(j)

        blocks = [(r, e) for r in range(2) for e in range(2)]

        def scores(r, e):
            query = qb[r * half:(r + 1) * half, pl.ds(pl.multiple_of(j * PAIR + e * NOPE, 128), WIDE)]
            key = kx[:, pl.ds(pl.multiple_of((j * 2 + e) * WIDE, 128), WIDE)]
            return lax.dot_general(key, query, NT, preferred_element_type=jnp.float32)

        ahead = scores(*blocks[0])
        for i, (r, e) in enumerate(blocks):
            s = ahead
            if i + 1 < len(blocks):
                ahead = scores(*blocks[i + 1])
            part = slice(r * half, (r + 1) * half)
            s = s + bias[:, part]
            peak = jnp.max(s, axis=0, keepdims=True)
            p = jnp.exp2(s - peak).astype(jnp.bfloat16)
            over = pl.ds(pl.multiple_of((j * 2 + e) * VDIM, 128), VDIM)
            both = jnp.concatenate([vt[over, :], ones], axis=0)
            acc = jnp.dot(both, p, preferred_element_type=jnp.float32)
            obuf[part, over] = (acc[:VDIM] / acc[VDIM:VDIM + 1]).T.astype(jnp.bfloat16)
        done = pl.ds(pl.multiple_of(j * 2 * VDIM, 128), 2 * VDIM)
        pltpu.make_async_copy(obuf.at[:, done], out_h.at[:, done], osem.at[j]).start()

        @pl.when((j + 1 >= early) & (j + 1 < pieces))
        def _():
            hand_on(j + 1)

        @pl.when(j + started < pieces)
        def _():
            for d in range(1, Y):
                y_copy(j + started - LAG, d).wait_send()
            start_piece(j + started)

    for t in range(1, Z):
        @pl.when(sends_up(t))
        def _():
            up_copy(t).wait_send()

        @pl.when(sends_down(t))
        def _():
            down_copy(t).wait_send()
    for layer in range(Z):
        for dx in range(1, X):
            x_copy(layer, dx).wait_send()

    left -= set(range(started - LAG, pieces - LAG))
    for j in sorted(left):
        for d in range(1, Y):
            y_copy(j, d).wait_send()

    @pl.loop(0, pieces)
    def _(j):
        c_copy(j).wait_send()
        for d in range(1, Y):
            f_copy(j, d).wait_send()
        done = pl.ds(pl.multiple_of(j * 2 * VDIM, 128), 2 * VDIM)
        pltpu.make_async_copy(obuf.at[:, done], out_h.at[:, done], osem.at[j]).wait()


def per_device(Y, Z, X, query_latent, q_weight, key_absorb, value_up, branch_latent, lengths, row_depth):
    rows, rank = query_latent.shape
    cols = q_weight.shape[1]
    heads = key_absorb.shape[0]
    share = branch_latent.shape[1]
    length = share * Z * X
    pieces = cols // PAIR
    width = heads * VDIM
    bf = jnp.bfloat16
    dma = pltpu.SemaphoreType.DMA
    anywhere = pl.BlockSpec(memory_space=pl.ANY)
    return pl.pallas_call(
        functools.partial(kernel, Y, Z, X),
        out_shape=jax.ShapeDtypeStruct((rows, width), bf),
        in_specs=[anywhere] * 5 + [pl.BlockSpec(memory_space=pltpu.VMEM), pl.BlockSpec(memory_space=pltpu.SMEM)],
        out_specs=anywhere,
        scratch_shapes=[
            pltpu.VMEM((rank, cols), bf),
            pltpu.VMEM((rows, rank), bf),
            pltpu.VMEM((heads * NOPE, KVR), bf),
            pltpu.VMEM((heads, KVR, VDIM), bf),
            pltpu.VMEM((width, KVR), bf),
            pltpu.VMEM((length, KVR + ROPE), bf),
            pltpu.VMEM((length, heads * WIDE), bf),
            pltpu.VMEM((width, length), bf),
            pltpu.VMEM((rows, width), bf),
            pltpu.VMEM((rows, cols), bf),
            pltpu.VMEM((length, rows), jnp.float32),
            dma((Y - 1, pieces)), dma((Y - 1, pieces)),
            dma((pieces,)), dma((pieces,)),
            dma((Y - 1, pieces)), dma((Y - 1, pieces)),
            dma((Z - 1,)), dma((Z - 1,)), dma((Z - 1,)), dma((Z - 1,)),
            dma((Z, X - 1)), dma((Z, X - 1)),
            dma((4,)), dma((2 * heads,)), dma((pieces,)),
        ],
        compiler_params=pltpu.CompilerParams(
            collective_id=0, has_side_effects=True, vmem_limit_bytes=60 * 1024 * 1024),
    )(query_latent, q_weight, key_absorb.reshape(heads * NOPE, KVR), value_up,
      branch_latent.reshape(share, KVR + ROPE), row_depth.reshape(1, rows), lengths)


def solution(mesh):
    placed = (
        P("grp", None),
        P("grp", "head"),
        P("head", None, None),
        P("head", None, None),
        P("grp", "head", None),
        P("grp"),
        P("grp"),
    )
    across = math.isqrt(mesh.shape["head"] // 2)
    return jax.shard_map(
        functools.partial(per_device, mesh.shape["grp"] // 2, mesh.shape["head"] // across, across),
        mesh=mesh, in_specs=placed, out_specs=P("grp", "head"), check_vma=False
    )
```
